32 devices in a mesh: rep: 8 (over z, x), shard: 4 (over y, core).
Axes of the slice: x: 2, y: 2, z: 4, core: 2. Of those that a mesh axis runs over, the one named last changes fastest.
Arguments:
- grads: float32 [8, 8, 8, 5120], P('rep', 'shard'), may hold values from -1000 to 1000
- weight: float32 [8, 8, 5120], P('shard'), may hold values from -6 to 6
- moment_one: float32 [8, 8, 5120], P('shard', 'rep'), may hold values from -6 to 6
- moment_two: float32 [8, 8, 5120], P('shard', 'rep'), may hold values from 0.1 to 3
Outputs:
- new_weight: float32 [8, 8, 5120], P('shard')
- new_moment_one: float32 [8, 8, 5120], P('shard', 'rep')
- new_moment_two: float32 [8, 8, 5120], P('shard', 'rep')
The draws below stay inside these ranges and needn't reach their ends.
All inputs are finite; a program needn't handle non-finite values.
Results may differ from the reference program's by a relative error of at most 0.0003.
Values sent between devices are 32-bit elements; how exact they have to be, the bound alone decides.
No kernel may reach another device: no remote copies, remote signals or barrier semaphores. Data moves between devices by JAX's collectives and lax.ppermute only.
A program may use at most 64 MiB of HBM per device.

```python
import math
import jax
import jax.numpy as jnp
from jax import lax

COLS = 5120
STEP = 100
REPLICAS = 8
TRIM = 1
SROWS = 8
RROWS = 8
PARAMS = 327680


def draw_grads(key, part):
    keys = jax.random.split(key, 7)
    first = jnp.arange(SROWS, dtype=jnp.float32) / max(SROWS - 1, 1)
    second = jnp.arange(RROWS, dtype=jnp.float32) / max(RROWS - 1, 1)
    rough = jax.random.uniform(keys[0], (SROWS, RROWS), jnp.float32, 0.7, 1.4)
    row_scale = (3.0 ** first)[:, None] * (3.3 ** second)[None, :] * rough
    col_scale = jnp.exp(jax.random.uniform(keys[1], (COLS,), jnp.float32, -0.693, 0.693))
    scale = row_scale[:, :, None] * col_scale[None, None, :]
    common = jnp.clip(jax.random.normal(keys[2], (SROWS, RROWS, COLS), jnp.float32), -5.0, 5.0) * scale
    noise = 1.5 * jnp.clip(jax.random.normal(keys[3], (REPLICAS, SROWS, RROWS, COLS), jnp.float32), -5.0, 5.0)
    flips = jax.random.uniform(keys[4], (REPLICAS, SROWS, RROWS, COLS), jnp.float32) < 0.0625
    signs = jnp.where(jax.random.uniform(keys[5], (REPLICAS, SROWS, RROWS, COLS), jnp.float32) < 0.5, -20.0, 20.0)
    outlier = jnp.where(flips, signs, 0.0)
    values = common[None] + (noise + outlier) * scale[None]
    shape = (REPLICAS, SROWS, RROWS, COLS)
    replica_index = lax.broadcasted_iota(jnp.int32, shape, 0)
    copy_mark = jax.random.randint(keys[6], shape, 0, 4) == 0
    own_value = jnp.logical_not(copy_mark) | (replica_index == 0)
    source = lax.cummax(jnp.where(own_value, replica_index, jnp.zeros_like(replica_index)), axis=0)
    return jnp.take_along_axis(values, source, axis=0)


def block_scale(own_key, extent, pieces, smallest, largest):
    factor_of, own = 1.0, jax.random.fold_in(own_key, 6)
    for position, shards_of in pieces:
        draws = jnp.exp(jax.random.uniform(jax.random.fold_in(own, position), (shards_of,), jnp.float32, smallest / len(pieces), largest / len(pieces)))
        factor_of = factor_of * jnp.repeat(draws, extent[position] // shards_of).reshape([-1 if axis == position else 1 for axis in range(len(extent))])
    return factor_of


def centred(key, extent, spread, bound, pieces=(), kind=jnp.bfloat16):
    gain = block_scale(key, extent, pieces, -0.22, 0.18) if pieces else 1.0
    drawn = jax.random.normal(key, extent, jnp.float32) * spread * gain
    return jnp.minimum(jnp.maximum(drawn, -bound), bound).astype(kind)


def setup_inputs(seed: int = 0) -> dict:
    key_list = jax.random.split(jax.random.key(seed), 5)
    grads = draw_grads(jax.random.fold_in(key_list[4], 71), 0)
    weight = centred(key_list[1], (SROWS, RROWS, COLS), 1.0, 6.0, ((0, 4),), jnp.float32)
    moment_one = centred(key_list[2], (SROWS, RROWS, COLS), 1.0, 6.0, ((0, 4), (1, 8)), jnp.float32)
    moment_two = jnp.clip(jnp.exp(math.log(3.0) - 3.4011974 * jax.random.uniform(key_list[3], (SROWS, RROWS, COLS), jnp.float32) ** block_scale(key_list[3], (SROWS, RROWS, COLS), ((0, 4), (1, 8)), -0.2, 0.2)), 0.1, 3.0)
    return {"grads": grads, "weight": weight, "moment_one": moment_one, "moment_two": moment_two}


def trimmed_block(block, trim_count):
    count = block.shape[0]
    order = jnp.arange(count, dtype=jnp.int32)
    lower = block[None, :, :] < block[:, None, :]
    equal = (block[None, :, :] == block[:, None, :]) & (order[None, :, None] < order[:, None, None])
    rank = lax.optimization_barrier(jnp.sum((lower | equal).astype(jnp.int32), axis=1))
    keep = (rank >= trim_count) & (rank < count - trim_count)
    kept = lax.optimization_barrier(jnp.sum(jnp.where(keep, block, jnp.zeros_like(block)), axis=0))
    return kept / (count - 2 * trim_count)

def trimmed_mean(values, trim_count):
    count, total = values.shape
    width = 512 if total % 512 == 0 else total
    blocks = values.reshape(count, total // width, width).transpose(1, 0, 2)
    result = lax.map(lambda item: trimmed_block(item, trim_count), blocks)
    return result.reshape(total)

def reference(grads, weight, moment_one, moment_two):
    flat = grads.reshape(grads.shape[0], -1)
    trimmed = trimmed_mean(flat, TRIM).reshape(weight.shape)
    total = jnp.sum(trimmed * trimmed)
    factor = jnp.minimum(1.0, 1.0 / jnp.sqrt(total / PARAMS + 1e-12))
    clipped = factor * trimmed
    new_one = 0.9 * moment_one + 0.1 * clipped
    new_two = 0.95 * moment_two + 0.05 * clipped * clipped
    update = new_one / (1.0 - 0.9 ** STEP) / (jnp.sqrt(new_two / (1.0 - 0.95 ** STEP)) + 1e-08)
    new_weight = weight - 0.05 * (update + 0.1 * weight)
    return (new_weight, new_one, new_two)
```

```python
import functools

import jax
import jax.numpy as jnp
from jax import lax
from jax.experimental import pallas as pl
from jax.experimental.pallas import tpu as pltpu
from jax.sharding import PartitionSpec as P

STEP = 100
LANES = 128
SUB = 8
VMEM = pl.BlockSpec(memory_space=pltpu.VMEM)


def f32(*shape):
    return jax.ShapeDtypeStruct(shape, jnp.float32)


def call(kernel, outs, args, scratch=()):
    return pl.pallas_call(
        kernel,
        out_shape=outs,
        in_specs=[VMEM] * len(args),
        out_specs=jax.tree.map(lambda _: VMEM, outs),
        scratch_shapes=scratch,
        compiler_params=pltpu.CompilerParams(vmem_limit_bytes=32 << 20),
    )(*args)


def middle_sum(values, trim):
    low, high, total = [], [], None
    for value in values:
        for place in reversed(range(len(low))):
            low[place], value = jnp.minimum(low[place], value), jnp.maximum(low[place], value)
        if len(low) < trim:
            low.append(value)
            continue
        for place in range(len(high)):
            value, high[place] = jnp.minimum(high[place], value), jnp.maximum(high[place], value)
        if len(high) < trim:
            high.insert(0, value)
            continue
        total = value if total is None else total + value
    return total


def pack_kernel(block_ref, out_ref):
    blocks, rows, cols = block_ref.shape
    tiles = cols // LANES
    run = blocks * tiles
    for b in range(blocks):
        for r in range(0, rows, SUB):
            for j in range(tiles):
                tile = block_ref[b, r : r + SUB, j * LANES : (j + 1) * LANES]
                out_ref[pl.ds(r * run + b * tiles + j, SUB, stride=run), :] = tile


def unpack_kernel(dense_ref, out_ref):
    blocks, rows, cols = out_ref.shape
    tiles = cols // LANES
    run = blocks * tiles
    for b in range(blocks):
        for r in range(0, rows, SUB):
            for j in range(tiles):
                out_ref[b, r : r + SUB, j * LANES : (j + 1) * LANES] = dense_ref[
                    pl.ds(r * run + b * tiles + j, SUB, stride=run), :
                ]


def trim_kernel(count, trim, received_ref, trimmed_ref, squares_ref):
    run = trimmed_ref.shape[0]
    squares = jnp.zeros((SUB, LANES), jnp.float32)
    for at in range(0, run, SUB):
        values = [received_ref[i * run + at : i * run + at + SUB, :] for i in range(count)]
        mean = middle_sum(values, trim) / (count - 2 * trim)
        trimmed_ref[at : at + SUB, :] = mean
        squares += mean * mean
    for at in range(0, squares_ref.shape[0], SUB):
        squares_ref[at : at + SUB, :] = squares


def clip_factor(squares_ref, params):
    squares = squares_ref[0:SUB, :]
    for at in range(SUB, squares_ref.shape[0], SUB):
        squares += squares_ref[at : at + SUB, :]
    total = jnp.sum(squares, keepdims=True)
    return jnp.minimum(1.0, 1.0 / jnp.sqrt(total / params + 1e-12))


def adam(factor, trimmed, one, two, weight):
    clipped = factor * trimmed
    new_one = 0.9 * one + 0.1 * clipped
    new_two = 0.95 * two + 0.05 * clipped * clipped
    update = new_one / (1.0 - 0.9**STEP) / (jnp.sqrt(new_two / (1.0 - 0.95**STEP)) + 1e-08)
    return weight - 0.05 * (update + 0.1 * weight), new_one, new_two


def adam_kernel(params, squares_ref, trimmed_ref, one_ref, two_ref, weight_ref, new_ref, new_one_ref, new_two_ref):
    factor = clip_factor(squares_ref, params)
    weight, one, two = adam(factor, trimmed_ref[...], one_ref[...], two_ref[...], weight_ref[...])
    new_one_ref[...] = one
    new_two_ref[...] = two
    run = trimmed_ref.shape[0]
    for at in range(0, new_ref.shape[0], run):
        new_ref[at : at + run, :] = weight


def on_device(grads, weight, moment_one, moment_two):
    count, shards = lax.axis_size("rep"), lax.axis_size("shard")
    blocks, rows, cols = weight.shape
    params = blocks * shards * rows * cols
    run = blocks * (rows // count) * cols // LANES
    everyone = count * shards

    packed = call(pack_kernel, f32(count * run, LANES), (grads[0],))
    received = lax.all_to_all(packed, "rep", 0, 0, tiled=True)
    trimmed, squares = call(
        functools.partial(trim_kernel, count, count // 8),
        (f32(run, LANES), f32(everyone * SUB, LANES)),
        (received,),
    )
    squares = lax.all_to_all(squares, ("rep", "shard"), 0, 0, tiled=True)
    owned = lax.dynamic_slice_in_dim(weight, lax.axis_index("rep") * moment_one.shape[1], moment_one.shape[1], 1)
    new, one, two = call(
        functools.partial(adam_kernel, params),
        (f32(count * run, LANES), f32(run, LANES), f32(run, LANES)),
        (squares, trimmed, moment_one.reshape(run, LANES), moment_two.reshape(run, LANES), owned.reshape(run, LANES)),
    )
    gathered = lax.all_to_all(new, "rep", 0, 0, tiled=True)
    new_weight = call(unpack_kernel, f32(*weight.shape), (gathered,))
    return new_weight, one.reshape(moment_one.shape), two.reshape(moment_two.shape)


def solution(mesh):
    return jax.shard_map(
        on_device,
        mesh=mesh,
        in_specs=(
            P("rep", "shard", None, None),
            P("shard", None, None),
            P("shard", "rep", None),
            P("shard", "rep", None),
        ),
        out_specs=(P("shard", None, None), P("shard", "rep", None), P("shard", "rep", None)),
        check_vma=False,
    )
```

```python
import functools

import jax
import jax.numpy as jnp
from jax import lax
from jax.experimental import pallas as pl
from jax.experimental.pallas import tpu as pltpu
from jax.sharding import PartitionSpec as P

STEP = 100
LANES = 128
SUB = 8
VMEM = pl.BlockSpec(memory_space=pltpu.VMEM)
SMEM = pl.BlockSpec(memory_space=pltpu.SMEM)
PARAMS = pltpu.CompilerParams(vmem_limit_bytes=32 << 20)


def f32(*shape):
    return jax.ShapeDtypeStruct(shape, jnp.float32)


def middle_sum(values, trim):
    low, high, total = [], [], None
    for value in values:
        for place in reversed(range(len(low))):
            low[place], value = jnp.minimum(low[place], value), jnp.maximum(low[place], value)
        if len(low) < trim:
            low.append(value)
            continue
        for place in range(len(high)):
            value, high[place] = jnp.minimum(high[place], value), jnp.maximum(high[place], value)
        if len(high) < trim:
            high.insert(0, value)
            continue
        total = value if total is None else total + value
    return total


def trim_kernel(trim, received_ref, trimmed_ref):
    count, tiles = received_ref.shape[:2]
    for tile in range(tiles):
        values = [received_ref[i, tile] for i in range(count)]
        mean = middle_sum(values, trim) / (count - 2 * trim)
        for i in range(count):
            trimmed_ref[i, tile] = mean


def square_kernel(trimmed_ref, squares_ref):
    squares = jnp.zeros((SUB, LANES), jnp.float32)
    for owner in range(trimmed_ref.shape[0]):
        for tile in range(trimmed_ref.shape[1]):
            squares += trimmed_ref[owner, tile] * trimmed_ref[owner, tile]
    squares_ref[...] = squares


def adam(factor, trimmed, one, two, weight):
    clipped = factor * trimmed
    new_one = 0.9 * one + 0.1 * clipped
    new_two = 0.95 * two + 0.05 * clipped * clipped
    update = new_one / (1.0 - 0.9**STEP) / (jnp.sqrt(new_two / (1.0 - 0.95**STEP)) + 1e-08)
    return weight - 0.05 * (update + 0.1 * weight), new_one, new_two


def adam_kernel(params, orders, me_ref, squares_ref, trimmed_ref, weight_ref, *refs):
    moment_refs, (new_ref, new_one_ref, new_two_ref, moments) = refs[: len(orders)], refs[len(orders) :]
    total = jnp.sum(squares_ref[...], keepdims=True)
    factor = jnp.minimum(1.0, 1.0 / jnp.sqrt(total / params + 1e-12))
    blocks, rows, cols = weight_ref.shape
    across = cols // LANES
    run = blocks * across
    me = me_ref[0]
    for order, ref in zip(orders, moment_refs):
        for part, place in enumerate(order):
            row = pl.multiple_of((me ^ place) * 2 * run, 2 * run)
            moments[pl.ds(row, 2 * run), :] = ref[part * 2 * run : (part + 1) * 2 * run, :]
    start = (me // SUB) * across * SUB + me % SUB
    own = moment_refs[0]
    for b in range(blocks):
        base = b * (rows // SUB) * across * SUB
        mine = trimmed_ref[pl.ds(base + start, across, stride=SUB), :]
        here, there = slice(b * across, (b + 1) * across), slice(run + b * across, run + (b + 1) * across)
        _, new_one_ref[here, :], new_two_ref[here, :] = adam(factor, mine, own[here, :], own[there, :], mine)
    tile = 0
    for b in range(blocks):
        for r in range(0, rows, SUB):
            for j in range(across):
                at = b * across + j
                trimmed = trimmed_ref[tile * SUB : (tile + 1) * SUB, :]
                one = moments[pl.ds(2 * r * run + at, SUB, stride=2 * run), :]
                two = moments[pl.ds((2 * r + 1) * run + at, SUB, stride=2 * run), :]
                lanes = slice(j * LANES, (j + 1) * LANES)
                new_ref[b, r : r + SUB, lanes], _, _ = adam(factor, trimmed, one, two, weight_ref[b, r : r + SUB, lanes])
                tile += 1


def on_device(grads, weight, moment_one, moment_two):
    count, shards = lax.axis_size("rep"), lax.axis_size("shard")
    blocks, rows, cols = weight.shape
    params = blocks * shards * rows * cols
    run = blocks * cols // LANES
    tiles = blocks * rows * cols // (SUB * LANES) // count

    def swap(value, axis, mask):
        return lax.ppermute(value, axis, [(i, i ^ mask) for i in range(lax.axis_size(axis))])

    tiled = grads.reshape(blocks, rows // SUB, SUB, cols // LANES, LANES).transpose(0, 1, 3, 2, 4)
    received = lax.all_to_all(tiled.reshape(count, tiles, SUB, LANES), "rep", 0, 0, tiled=True)

    moments = [jnp.concatenate([moment_one.reshape(run, LANES), moment_two.reshape(run, LANES)])]
    orders = [[0]]
    masks = [1, 4, 2]

    def spread(mask):
        held = moments[0] if len(moments) == 1 else jnp.concatenate(moments)
        orders.append([place ^ mask for order in orders for place in order])
        moments.append(swap(held, "rep", mask))

    spread(masks[0])
    received, moments[-1] = lax.optimization_barrier((received, moments[-1]))
    spread(masks[1])
    spread(masks[2])
    trimmed = pl.pallas_call(
        functools.partial(trim_kernel, count // 8),
        out_shape=f32(count, tiles, SUB, LANES),
        in_specs=[VMEM],
        out_specs=VMEM,
        compiler_params=PARAMS,
    )(received)
    trimmed = lax.all_to_all(trimmed, "rep", 0, 0, tiled=True)
    squares = pl.pallas_call(
        square_kernel, out_shape=f32(SUB, LANES), in_specs=[VMEM], out_specs=VMEM, compiler_params=PARAMS
    )(trimmed)
    mask = 1
    while mask < shards:
        squares += swap(squares, "shard", mask)
        mask *= 2
    args = (lax.axis_index("rep").reshape(1), squares, trimmed.reshape(-1, LANES), weight, *moments)
    new_weight, one, two = pl.pallas_call(
        functools.partial(adam_kernel, params, orders),
        out_shape=(f32(*weight.shape), f32(run, LANES), f32(run, LANES)),
        in_specs=[SMEM] + [VMEM] * (len(args) - 1),
        out_specs=(VMEM, VMEM, VMEM),
        scratch_shapes=[pltpu.VMEM((count * 2 * run, LANES), jnp.float32)],
        compiler_params=PARAMS,
    )(*args)
    return new_weight, one.reshape(moment_one.shape), two.reshape(moment_two.shape)


def solution(mesh):
    return jax.shard_map(
        on_device,
        mesh=mesh,
        in_specs=(
            P("rep", "shard", None, None),
            P("shard", None, None),
            P("shard", "rep", None),
            P("shard", "rep", None),
        ),
        out_specs=(P("shard", None, None), P("shard", "rep", None), P("shard", "rep", None)),
        check_vma=False,
    )
```

```python
import functools

import jax
import jax.numpy as jnp
from jax import lax
from jax.experimental import pallas as pl
from jax.experimental.pallas import tpu as pltpu
from jax.sharding import PartitionSpec as P

STEP = 100
LANES = 128
SUB = 8
VMEM = pl.BlockSpec(memory_space=pltpu.VMEM)
SMEM = pl.BlockSpec(memory_space=pltpu.SMEM)
PARAMS = pltpu.CompilerParams(vmem_limit_bytes=32 << 20)


def f32(*shape):
    return jax.ShapeDtypeStruct(shape, jnp.float32)


def middle_sum(values, trim):
    low, high, total = [], [], None
    for value in values:
        for place in reversed(range(len(low))):
            low[place], value = jnp.minimum(low[place], value), jnp.maximum(low[place], value)
        if len(low) < trim:
            low.append(value)
            continue
        for place in range(len(high)):
            value, high[place] = jnp.minimum(high[place], value), jnp.maximum(high[place], value)
        if len(high) < trim:
            high.insert(0, value)
            continue
        total = value if total is None else total + value
    return total


def trim_kernel(trim, received_ref, trimmed_ref):
    count, tiles = received_ref.shape[:2]
    for tile in range(tiles):
        values = [received_ref[i, tile] for i in range(count)]
        mean = middle_sum(values, trim) / (count - 2 * trim)
        for i in range(count):
            trimmed_ref[i, tile] = mean


def square_kernel(trimmed_ref, squares_ref):
    squares = jnp.zeros((SUB, LANES), jnp.float32)
    for owner in range(trimmed_ref.shape[0]):
        for tile in range(trimmed_ref.shape[1]):
            squares += trimmed_ref[owner, tile] * trimmed_ref[owner, tile]
    squares_ref[...] = squares


def adam(factor, trimmed, one, two, weight):
    clipped = factor * trimmed
    new_one = 0.9 * one + 0.1 * clipped
    new_two = 0.95 * two + 0.05 * clipped * clipped
    update = new_one / (1.0 - 0.9**STEP) / (jnp.sqrt(new_two / (1.0 - 0.95**STEP)) + 1e-08)
    return weight - 0.05 * (update + 0.1 * weight), new_one, new_two


def adam_kernel(params, orders, me_ref, squares_ref, trimmed_ref, weight_ref, *refs):
    moment_refs, (new_ref, new_one_ref, new_two_ref, moments) = refs[: len(orders)], refs[len(orders) :]
    total = jnp.sum(squares_ref[...], keepdims=True)
    factor = jnp.minimum(1.0, 1.0 / jnp.sqrt(total / params + 1e-12))
    blocks, rows, cols = weight_ref.shape
    across = cols // LANES
    run = blocks * across
    me = me_ref[0]
    for order, ref in zip(orders, moment_refs):
        for part, place in enumerate(order):
            row = pl.multiple_of((me ^ place) * 2 * run, 2 * run)
            moments[pl.ds(row, 2 * run), :] = ref[part * 2 * run : (part + 1) * 2 * run, :]
    start = (me // SUB) * across * SUB + me % SUB
    own = moment_refs[0]
    for b in range(blocks):
        base = b * (rows // SUB) * across * SUB
        mine = trimmed_ref[pl.ds(base + start, across, stride=SUB), :]
        here, there = slice(b * across, (b + 1) * across), slice(run + b * across, run + (b + 1) * across)
        _, new_one_ref[here, :], new_two_ref[here, :] = adam(factor, mine, own[here, :], own[there, :], mine)
    tile = 0
    for b in range(blocks):
        for r in range(0, rows, SUB):
            for j in range(across):
                at = b * across + j
                trimmed = trimmed_ref[tile * SUB : (tile + 1) * SUB, :]
                one = moments[pl.ds(2 * r * run + at, SUB, stride=2 * run), :]
                two = moments[pl.ds((2 * r + 1) * run + at, SUB, stride=2 * run), :]
                lanes = slice(j * LANES, (j + 1) * LANES)
                new_ref[b, r : r + SUB, lanes], _, _ = adam(factor, trimmed, one, two, weight_ref[b, r : r + SUB, lanes])
                tile += 1


def on_device(grads, weight, moment_one, moment_two):
    count, shards = lax.axis_size("rep"), lax.axis_size("shard")
    blocks, rows, cols = weight.shape
    params = blocks * shards * rows * cols
    run = blocks * cols // LANES
    tiles = blocks * rows * cols // (SUB * LANES) // count

    def swap(value, axis, mask):
        return lax.ppermute(value, axis, [(i, i ^ mask) for i in range(lax.axis_size(axis))])

    tiled = grads.reshape(blocks, rows // SUB, SUB, cols // LANES, LANES).transpose(0, 1, 3, 2, 4)
    received = lax.all_to_all(tiled.reshape(count, tiles, SUB, LANES), "rep", 0, 0, tiled=True)

    moments = [jnp.concatenate([moment_one.reshape(run, LANES), moment_two.reshape(run, LANES)])]
    orders = [[0]]
    masks = [1 << bit for bit in range(1, (count - 1).bit_length())] + [1]

    def spread(mask):
        held = moments[0] if len(moments) == 1 else jnp.concatenate(moments)
        orders.append([place ^ mask for order in orders for place in order])
        moments.append(swap(held, "rep", mask))

    for mask in masks[:]:
        spread(mask)
    trimmed = pl.pallas_call(
        functools.partial(trim_kernel, count // 8),
        out_shape=f32(count, tiles, SUB, LANES),
        in_specs=[VMEM],
        out_specs=VMEM,
        compiler_params=PARAMS,
    )(received)
    trimmed = lax.all_to_all(trimmed, "rep", 0, 0, tiled=True)
    squares = pl.pallas_call(
        square_kernel, out_shape=f32(SUB, LANES), in_specs=[VMEM], out_specs=VMEM, compiler_params=PARAMS
    )(trimmed)
    mask = 1
    while mask < shards:
        squares += swap(squares, "shard", mask)
        mask *= 2
    args = (lax.axis_index("rep").reshape(1), squares, trimmed.reshape(-1, LANES), weight, *moments)
    new_weight, one, two = pl.pallas_call(
        functools.partial(adam_kernel, params, orders),
        out_shape=(f32(*weight.shape), f32(run, LANES), f32(run, LANES)),
        in_specs=[SMEM] + [VMEM] * (len(args) - 1),
        out_specs=(VMEM, VMEM, VMEM),
        scratch_shapes=[pltpu.VMEM((count * 2 * run, LANES), jnp.float32)],
        compiler_params=PARAMS,
    )(*args)
    return new_weight, one.reshape(moment_one.shape), two.reshape(moment_two.shape)


def solution(mesh):
    return jax.shard_map(
        on_device,
        mesh=mesh,
        in_specs=(
            P("rep", "shard", None, None),
            P("shard", None, None),
            P("shard", "rep", None),
            P("shard", "rep", None),
        ),
        out_specs=(P("shard", None, None), P("shard", "rep", None), P("shard", "rep", None)),
        check_vma=False,
    )
```

```python
import functools

import jax
import jax.numpy as jnp
from jax import lax
from jax.experimental import pallas as pl
from jax.experimental.pallas import tpu as pltpu
from jax.sharding import PartitionSpec as P

STEP = 100
LANES = 128
SUB = 8
VMEM = pl.BlockSpec(memory_space=pltpu.VMEM)
SMEM = pl.BlockSpec(memory_space=pltpu.SMEM)
PARAMS = pltpu.CompilerParams(vmem_limit_bytes=32 << 20)


def f32(*shape):
    return jax.ShapeDtypeStruct(shape, jnp.float32)


def middle_sum(values, trim):
    low, high, total = [], [], None
    for value in values:
        for place in reversed(range(len(low))):
            low[place], value = jnp.minimum(low[place], value), jnp.maximum(low[place], value)
        if len(low) < trim:
            low.append(value)
            continue
        for place in range(len(high)):
            value, high[place] = jnp.minimum(high[place], value), jnp.maximum(high[place], value)
        if len(high) < trim:
            high.insert(0, value)
            continue
        total = value if total is None else total + value
    return total


def trim_kernel(trim, received_ref, trimmed_ref):
    count, tiles = received_ref.shape[:2]
    for tile in range(tiles):
        values = [received_ref[i, tile] for i in range(count)]
        mean = middle_sum(values, trim) / (count - 2 * trim)
        for i in range(count):
            trimmed_ref[i, tile] = mean


def square_kernel(trimmed_ref, squares_ref):
    squares = jnp.zeros((SUB, LANES), jnp.float32)
    for owner in range(trimmed_ref.shape[0]):
        for tile in range(trimmed_ref.shape[1]):
            squares += trimmed_ref[owner, tile] * trimmed_ref[owner, tile]
    squares_ref[...] = squares


def spread_kernel(orders, me_ref, weight_ref, *refs):
    moment_refs, (one_ref, two_ref, kept_ref, moments) = refs[: len(orders)], refs[len(orders) :]
    blocks, rows, cols = weight_ref.shape
    across = cols // LANES
    run = blocks * across
    me = me_ref[0]
    for order, ref in zip(orders, moment_refs):
        for part, place in enumerate(order):
            row = pl.multiple_of((me ^ place) * 2 * run, 2 * run)
            moments[pl.ds(row, 2 * run), :] = ref[part * 2 * run : (part + 1) * 2 * run, :]
    at = 0
    for b in range(blocks):
        for r in range(0, rows, SUB):
            for j in range(across):
                col = b * across + j
                one_ref[at : at + SUB, :] = 0.9 * moments[pl.ds(2 * r * run + col, SUB, stride=2 * run), :]
                two_ref[at : at + SUB, :] = 0.95 * moments[pl.ds((2 * r + 1) * run + col, SUB, stride=2 * run), :]
                weight = weight_ref[b, r : r + SUB, j * LANES : (j + 1) * LANES]
                kept_ref[at : at + SUB, :] = weight - 0.05 * (0.1 * weight)
                at += SUB


def adam_kernel(params, me_ref, squares_ref, trimmed_ref, ones_ref, twos_ref, kept_ref, own_ref, new_ref, new_one_ref, new_two_ref):
    total = jnp.sum(squares_ref[...], keepdims=True)
    factor = jnp.minimum(1.0, 1.0 / jnp.sqrt(total / params + 1e-12))
    blocks, rows, cols = new_ref.shape
    across = cols // LANES
    run = blocks * across
    me = me_ref[0]
    start = (me // SUB) * across * SUB + me % SUB
    for b in range(blocks):
        base = b * (rows // SUB) * across * SUB
        clipped = factor * trimmed_ref[pl.ds(base + start, across, stride=SUB), :]
        here = slice(b * across, (b + 1) * across)
        new_one_ref[here, :] = 0.9 * own_ref[here, :] + 0.1 * clipped
        there = slice(run + b * across, run + (b + 1) * across)
        new_two_ref[here, :] = 0.95 * own_ref[there, :] + 0.05 * clipped * clipped
    at = 0
    for b in range(blocks):
        for r in range(0, rows, SUB):
            for j in range(across):
                tile = slice(at, at + SUB)
                clipped = factor * trimmed_ref[tile, :]
                one = ones_ref[tile, :] + 0.1 * clipped
                two = twos_ref[tile, :] + 0.05 * clipped * clipped
                update = one / (1.0 - 0.9**STEP) / (jnp.sqrt(two / (1.0 - 0.95**STEP)) + 1e-08)
                new_ref[b, r : r + SUB, j * LANES : (j + 1) * LANES] = kept_ref[tile, :] - 0.05 * update
                at += SUB


def on_device(grads, weight, moment_one, moment_two):
    count, shards = lax.axis_size("rep"), lax.axis_size("shard")
    blocks, rows, cols = weight.shape
    params = blocks * shards * rows * cols
    run = blocks * cols // LANES
    tiles = blocks * rows * cols // (SUB * LANES) // count

    def swap(value, axis, mask):
        return lax.ppermute(value, axis, [(i, i ^ mask) for i in range(lax.axis_size(axis))])

    tiled = grads.reshape(blocks, rows // SUB, SUB, cols // LANES, LANES).transpose(0, 1, 3, 2, 4)
    received = lax.all_to_all(tiled.reshape(count, tiles, SUB, LANES), "rep", 0, 0, tiled=True)

    moments = [jnp.concatenate([moment_one.reshape(run, LANES), moment_two.reshape(run, LANES)])]
    orders = [[0]]
    masks = [2] + [3 << bit for bit in range(1, (count - 1).bit_length() - 1)] + [1]

    def spread(mask):
        held = moments[0] if len(moments) == 1 else jnp.concatenate(moments)
        orders.append([place ^ mask for order in orders for place in order])
        moments.append(swap(held, "rep", mask))

    for mask in masks:
        spread(mask)
    trimmed = pl.pallas_call(
        functools.partial(trim_kernel, count // 8),
        out_shape=f32(count, tiles, SUB, LANES),
        in_specs=[VMEM],
        out_specs=VMEM,
        compiler_params=PARAMS,
    )(received)
    trimmed = lax.all_to_all(trimmed, "rep", 0, 0, tiled=True)
    squares = pl.pallas_call(
        square_kernel, out_shape=f32(SUB, LANES), in_specs=[VMEM], out_specs=VMEM, compiler_params=PARAMS
    )(trimmed)
    for mask in [1] + [(1 << bit) + 1 for bit in range(1, (shards - 1).bit_length())]:
        squares += swap(squares, "shard", mask)
    me = lax.axis_index("rep").reshape(1)
    ready = f32(weight.size // LANES, LANES)
    decayed = pl.pallas_call(
        functools.partial(spread_kernel, orders),
        out_shape=(ready, ready, ready),
        in_specs=[SMEM] + [VMEM] * (1 + len(moments)),
        out_specs=(VMEM, VMEM, VMEM),
        scratch_shapes=[pltpu.VMEM((count * 2 * run, LANES), jnp.float32)],
        compiler_params=PARAMS,
    )(me, weight, *moments)
    new_weight, one, two = pl.pallas_call(
        functools.partial(adam_kernel, params),
        out_shape=(f32(*weight.shape), f32(run, LANES), f32(run, LANES)),
        in_specs=[SMEM] + [VMEM] * 6,
        out_specs=(VMEM, VMEM, VMEM),
        compiler_params=PARAMS,
    )(me, squares, trimmed.reshape(-1, LANES), *decayed, moments[0])
    return new_weight, one.reshape(moment_one.shape), two.reshape(moment_two.shape)


def solution(mesh):
    return jax.shard_map(
        on_device,
        mesh=mesh,
        in_specs=(
            P("rep", "shard", None, None),
            P("shard", None, None),
            P("shard", "rep", None),
            P("shard", "rep", None),
        ),
        out_specs=(P("shard", None, None), P("shard", "rep", None), P("shard", "rep", None)),
        check_vma=False,
    )
```

```python
import functools
import operator

import jax
import jax.numpy as jnp
from jax import lax
from jax.experimental import pallas as pl
from jax.experimental.pallas import tpu as pltpu
from jax.sharding import PartitionSpec as P

STEP = 100
LANES = 128
SUB = 8
VMEM = pl.BlockSpec(memory_space=pltpu.VMEM)
SMEM = pl.BlockSpec(memory_space=pltpu.SMEM)
PARAMS = pltpu.CompilerParams(vmem_limit_bytes=32 << 20)


def f32(*shape):
    return jax.ShapeDtypeStruct(shape, jnp.float32)


def middle_sum(values, trim):
    low, high, total = [], [], None
    for value in values:
        for place in reversed(range(len(low))):
            low[place], value = jnp.minimum(low[place], value), jnp.maximum(low[place], value)
        if len(low) < trim:
            low.append(value)
            continue
        for place in range(len(high)):
            value, high[place] = jnp.minimum(high[place], value), jnp.maximum(high[place], value)
        if len(high) < trim:
            high.insert(0, value)
            continue
        total = value if total is None else total + value
    return total


def trim_kernel(trim, received_ref, trimmed_ref):
    count, tiles = received_ref.shape[:2]
    for tile in range(tiles):
        values = [received_ref[i, tile] for i in range(count)]
        mean = middle_sum(values, trim) / (count - 2 * trim)
        for i in range(count):
            trimmed_ref[i, tile] = mean


def square_kernel(trimmed_ref, squares_ref):
    squares = jnp.zeros((SUB, LANES), jnp.float32)
    for owner in range(trimmed_ref.shape[0]):
        for tile in range(trimmed_ref.shape[1]):
            squares += trimmed_ref[owner, tile] * trimmed_ref[owner, tile]
    squares_ref[...] = squares


def ready_kernel(shards, orders, at_ref, weight_ref, trimmed_ref, *refs):
    moment_refs, (kept_ref, one_ref, one_slope_ref, two_ref, two_slope_ref, own_ref, moments) = refs[: len(orders)], refs[len(orders) :]
    blocks, rows, cols = weight_ref.shape
    across = cols // LANES
    run = blocks * across
    me, core = at_ref[0] // shards, at_ref[0] % 2
    for order, ref in zip(orders, moment_refs):
        for part, place in enumerate(order):
            away = jnp.where(core == 0, place[0], place[1])
            row = pl.multiple_of((me ^ away) * 2 * run, 2 * run)
            moments[pl.ds(row, 2 * run), :] = ref[part * 2 * run : (part + 1) * 2 * run, :]
    start = (me // SUB) * across * SUB + me % SUB
    for b in range(blocks):
        base = b * (rows // SUB) * across * SUB
        own_ref[b * across : (b + 1) * across, :] = trimmed_ref[pl.ds(base + start, across, stride=SUB), :]
    one_scale, two_scale = 0.05 / (1.0 - 0.9**STEP), 1.0 / (1.0 - 0.95**STEP)
    at = 0
    for b in range(blocks):
        for r in range(0, rows, SUB):
            for j in range(across):
                col = b * across + j
                tile = slice(at, at + SUB)
                trimmed = trimmed_ref[tile, :]
                one = moments[pl.ds(2 * r * run + col, SUB, stride=2 * run), :]
                two = moments[pl.ds((2 * r + 1) * run + col, SUB, stride=2 * run), :]
                weight = weight_ref[b, r : r + SUB, j * LANES : (j + 1) * LANES]
                kept_ref[tile, :] = weight - 0.05 * (0.1 * weight)
                one_ref[tile, :] = (0.9 * one_scale) * one
                one_slope_ref[tile, :] = (0.1 * one_scale) * trimmed
                two_ref[tile, :] = (0.95 * two_scale) * two
                two_slope_ref[tile, :] = (0.05 * two_scale) * trimmed * trimmed
                at += SUB


def adam_kernel(params, squares_ref, kept_ref, one_ref, one_slope_ref, two_ref, two_slope_ref, own_ref, own_moments_ref, new_ref, new_one_ref, new_two_ref):
    total = jnp.sum(squares_ref[...], keepdims=True)
    factor = jnp.minimum(1.0, 1.0 / jnp.sqrt(total / params + 1e-12))
    square = factor * factor
    run = own_ref.shape[0]
    clipped = factor * own_ref[...]
    new_one_ref[...] = 0.9 * own_moments_ref[0:run, :] + 0.1 * clipped
    new_two_ref[...] = 0.95 * own_moments_ref[run : 2 * run, :] + 0.05 * clipped * clipped
    blocks, rows, cols = new_ref.shape
    at = 0
    for b in range(blocks):
        for r in range(0, rows, SUB):
            for j in range(cols // LANES):
                tile = slice(at, at + SUB)
                one = one_ref[tile, :] + factor * one_slope_ref[tile, :]
                two = two_ref[tile, :] + square * two_slope_ref[tile, :]
                new_ref[b, r : r + SUB, j * LANES : (j + 1) * LANES] = kept_ref[tile, :] - one / (jnp.sqrt(two) + 1e-08)
                at += SUB


def on_device(grads, weight, moment_one, moment_two):
    count, shards = lax.axis_size("rep"), lax.axis_size("shard")
    blocks, rows, cols = weight.shape
    params = blocks * shards * rows * cols
    run = blocks * cols // LANES
    tiles = blocks * rows * cols // (SUB * LANES) // count

    def swap(value, axis, mask):
        return lax.ppermute(value, axis, [(i, i ^ mask) for i in range(lax.axis_size(axis))])

    tiled = grads.reshape(blocks, rows // SUB, SUB, cols // LANES, LANES).transpose(0, 1, 3, 2, 4)
    received = lax.all_to_all(tiled.reshape(count, tiles, SUB, LANES), "rep", 0, 0, tiled=True)

    moments = [jnp.concatenate([moment_one.reshape(run, LANES), moment_two.reshape(run, LANES)])]
    orders = [[(0, 0)]]
    masks = list(zip([1, 6, 2], [2, 6, 1]))

    def spread(mask):
        held = moments[0] if len(moments) == 1 else jnp.concatenate(moments)
        orders.append([tuple(map(operator.xor, place, mask)) for order in orders for place in order])
        pairs = [(r * shards + s, (r ^ mask[s % 2]) * shards + s) for r in range(count) for s in range(shards)]
        moments.append(lax.ppermute(held, ("rep", "shard"), pairs))

    for mask in masks:
        spread(mask)
    trimmed = pl.pallas_call(
        functools.partial(trim_kernel, count // 8),
        out_shape=f32(count, tiles, SUB, LANES),
        in_specs=[VMEM],
        out_specs=VMEM,
        compiler_params=PARAMS,
    )(received)
    trimmed = lax.all_to_all(trimmed, "rep", 0, 0, tiled=True)
    squares = pl.pallas_call(
        square_kernel, out_shape=f32(SUB, LANES), in_specs=[VMEM], out_specs=VMEM, compiler_params=PARAMS
    )(trimmed)
    for mask in [1] + [(1 << bit) + 1 for bit in range(1, (shards - 1).bit_length())]:
        squares += swap(squares, "shard", mask)
    at = lax.axis_index(("rep", "shard")).reshape(1)
    flat = f32(weight.size // LANES, LANES)
    ready = pl.pallas_call(
        functools.partial(ready_kernel, shards, orders),
        out_shape=(flat,) * 5 + (f32(run, LANES),),
        in_specs=[SMEM] + [VMEM] * (2 + len(moments)),
        out_specs=(VMEM,) * 6,
        scratch_shapes=[pltpu.VMEM((count * 2 * run, LANES), jnp.float32)],
        compiler_params=PARAMS,
    )(at, weight, trimmed.reshape(-1, LANES), *moments)
    new_weight, one, two = pl.pallas_call(
        functools.partial(adam_kernel, params),
        out_shape=(f32(*weight.shape), f32(run, LANES), f32(run, LANES)),
        in_specs=[VMEM] * 8,
        out_specs=(VMEM,) * 3,
        compiler_params=PARAMS,
    )(squares, *ready, moments[0])
    return new_weight, one.reshape(moment_one.shape), two.reshape(moment_two.shape)


def solution(mesh):
    return jax.shard_map(
        on_device,
        mesh=mesh,
        in_specs=(
            P("rep", "shard", None, None),
            P("shard", None, None),
            P("shard", "rep", None),
            P("shard", "rep", None),
        ),
        out_specs=(P("shard", None, None), P("shard", "rep", None), P("shard", "rep", None)),
        check_vma=False,
    )
```

```python
import functools
import operator

import jax
import jax.numpy as jnp
from jax import lax
from jax.experimental import pallas as pl
from jax.experimental.pallas import tpu as pltpu
from jax.sharding import PartitionSpec as P

STEP = 100
LANES = 128
PARTS = 4
SUB = 8
VMEM = pl.BlockSpec(memory_space=pltpu.VMEM)
SMEM = pl.BlockSpec(memory_space=pltpu.SMEM)
PARAMS = pltpu.CompilerParams(vmem_limit_bytes=32 << 20)


def f32(*shape):
    return jax.ShapeDtypeStruct(shape, jnp.float32)


def middle_sum(values, trim):
    low, high, total = [], [], None
    for value in values:
        for place in reversed(range(len(low))):
            low[place], value = jnp.minimum(low[place], value), jnp.maximum(low[place], value)
        if len(low) < trim:
            low.append(value)
            continue
        for place in range(len(high)):
            value, high[place] = jnp.minimum(high[place], value), jnp.maximum(high[place], value)
        if len(high) < trim:
            high.insert(0, value)
            continue
        total = value if total is None else total + value
    return total


def trim_kernel(trim, received_ref, trimmed_ref):
    count, tiles = received_ref.shape[:2]
    for tile in range(tiles):
        values = [received_ref[i, tile] for i in range(count)]
        mean = middle_sum(values, trim) / (count - 2 * trim)
        for i in range(count):
            trimmed_ref[i, tile] = mean


def square_kernel(trimmed_ref, squares_ref):
    squares = jnp.zeros((SUB, LANES), jnp.float32)
    for owner in range(trimmed_ref.shape[0]):
        for tile in range(trimmed_ref.shape[1]):
            squares += trimmed_ref[owner, tile] * trimmed_ref[owner, tile]
    squares_ref[...] = squares


def ready_kernel(shards, orders, at_ref, weight_ref, trimmed_ref, *refs):
    moment_refs, (kept_ref, one_ref, one_slope_ref, two_ref, two_slope_ref, own_ref, moments) = refs[: len(orders)], refs[len(orders) :]
    blocks, rows, cols = weight_ref.shape
    across = cols // LANES
    run = blocks * across
    me, core = at_ref[0] // shards, at_ref[0] % 2
    for order, ref in zip(orders, moment_refs):
        for part, place in enumerate(order):
            away = jnp.where(core == 0, place[0], place[1])
            row = pl.multiple_of((me ^ away) * 2 * run, 2 * run)
            moments[pl.ds(row, 2 * run), :] = ref[part * 2 * run : (part + 1) * 2 * run, :]
    start = (me // SUB) * across * SUB + me % SUB
    for b in range(blocks):
        base = b * (rows // SUB) * across * SUB
        own_ref[b * across : (b + 1) * across, :] = trimmed_ref[pl.ds(base + start, across, stride=SUB), :]
    one_scale, two_scale = 0.05 / (1.0 - 0.9**STEP), 1.0 / (1.0 - 0.95**STEP)
    at = 0
    for b in range(blocks):
        for r in range(0, rows, SUB):
            for j in range(across):
                col = b * across + j
                tile = slice(at, at + SUB)
                trimmed = trimmed_ref[tile, :]
                one = moments[pl.ds(2 * r * run + col, SUB, stride=2 * run), :]
                two = moments[pl.ds((2 * r + 1) * run + col, SUB, stride=2 * run), :]
                weight = weight_ref[b, r : r + SUB, j * LANES : (j + 1) * LANES]
                kept_ref[tile, :] = weight - 0.05 * (0.1 * weight)
                one_ref[tile, :] = (0.9 * one_scale) * one
                one_slope_ref[tile, :] = (0.1 * one_scale) * trimmed
                two_ref[tile, :] = (0.95 * two_scale) * two
                two_slope_ref[tile, :] = (0.05 * two_scale) * trimmed * trimmed
                at += SUB


def adam_kernel(params, squares_ref, kept_ref, one_ref, one_slope_ref, two_ref, two_slope_ref, own_ref, own_moments_ref, *refs):
    outs, stages, done = refs[:3], refs[3:6], refs[6]
    new, new_one, new_two = stages
    total = jnp.sum(squares_ref[...], keepdims=True)
    factor = jnp.minimum(1.0, 1.0 / jnp.sqrt(total / params + 1e-12))
    square = factor * factor
    run = own_ref.shape[0]
    clipped = factor * own_ref[...]
    new_one[...] = 0.9 * own_moments_ref[0:run, :] + 0.1 * clipped
    new_two[...] = 0.95 * own_moments_ref[run : 2 * run, :] + 0.05 * clipped * clipped
    copies = [pltpu.make_async_copy(new_one, outs[1], done.at[0]), pltpu.make_async_copy(new_two, outs[2], done.at[1])]
    for copy in copies:
        copy.start()
    blocks, rows, cols = new.shape
    across = cols // LANES
    at = 0
    for b in range(blocks):
        for r in range(0, rows, SUB):
            for j in range(across):
                tile = slice(at, at + SUB)
                one = one_ref[tile, :] + factor * one_slope_ref[tile, :]
                two = two_ref[tile, :] + square * two_slope_ref[tile, :]
                new[b, r : r + SUB, j * LANES : (j + 1) * LANES] = kept_ref[tile, :] - one / (jnp.sqrt(two) + 1e-08)
                at += SUB
                if (j + 1) % (across // PARTS) == 0:
                    part = slice((j + 1 - across // PARTS) * LANES, (j + 1) * LANES)
                    place = (b, slice(r, r + SUB), part)
                    copies.append(pltpu.make_async_copy(new.at[place], outs[0].at[place], done.at[len(copies)]))
                    copies[-1].start()
    for copy in copies:
        copy.wait()


def from_middle(count):
    return sorted(range(count), key=lambda i: (i % 2, abs(40 * (i // 2) - 19 * (count // 2))))


def on_device(grads, weight, moment_one, moment_two):
    count, shards = lax.axis_size("rep"), lax.axis_size("shard")
    blocks, rows, cols = weight.shape
    params = blocks * shards * rows * cols
    run = blocks * cols // LANES
    tiles = blocks * rows * cols // (SUB * LANES) // count

    def swap(value, axis, mask):
        return lax.ppermute(value, axis, [(i, i ^ mask) for i in range(lax.axis_size(axis))])

    order = from_middle(count)
    tiled = grads.reshape(blocks, rows // SUB, SUB, cols // LANES, LANES).transpose(0, 1, 3, 2, 4)
    received = lax.all_to_all(tiled.reshape(count, tiles, SUB, LANES), "rep", 0, 0, tiled=True, axis_index_groups=[order])

    moments = [jnp.concatenate([moment_one.reshape(run, LANES), moment_two.reshape(run, LANES)])]
    orders = [[(0, 0)]]
    masks = list(zip([1, 6, 2], [2, 6, 1]))

    def spread(mask):
        held = moments[0] if len(moments) == 1 else jnp.concatenate(moments)
        orders.append([tuple(map(operator.xor, place, mask)) for order in orders for place in order])
        pairs = [(r * shards + s, (r ^ mask[s % 2]) * shards + s) for r in range(count) for s in range(shards)]
        moments.append(lax.ppermute(held, ("rep", "shard"), pairs))

    for mask in masks:
        spread(mask)
    trimmed = pl.pallas_call(
        functools.partial(trim_kernel, count // 8),
        out_shape=f32(count, tiles, SUB, LANES),
        in_specs=[VMEM],
        out_specs=VMEM,
        compiler_params=PARAMS,
    )(received)
    trimmed = lax.all_to_all(trimmed, "rep", 0, 0, tiled=True, axis_index_groups=[order])
    squares = pl.pallas_call(
        square_kernel, out_shape=f32(SUB, LANES), in_specs=[VMEM], out_specs=VMEM, compiler_params=PARAMS
    )(trimmed)
    for mask in [1] + [(1 << bit) + 1 for bit in range(1, (shards - 1).bit_length())]:
        squares += swap(squares, "shard", mask)
    at = lax.axis_index(("rep", "shard")).reshape(1)
    flat = f32(weight.size // LANES, LANES)
    ready = pl.pallas_call(
        functools.partial(ready_kernel, shards, orders),
        out_shape=(flat,) * 5 + (f32(run, LANES),),
        in_specs=[SMEM] + [VMEM] * (2 + len(moments)),
        out_specs=(VMEM,) * 6,
        scratch_shapes=[pltpu.VMEM((count * 2 * run, LANES), jnp.float32)],
        compiler_params=PARAMS,
    )(at, weight, trimmed.reshape(-1, LANES), *moments)
    new_weight, one, two = pl.pallas_call(
        functools.partial(adam_kernel, params),
        out_shape=(f32(*weight.shape), f32(run, LANES), f32(run, LANES)),
        in_specs=[VMEM] * 8,
        out_specs=(pl.BlockSpec(memory_space=pl.ANY),) * 3,
        scratch_shapes=[
            pltpu.VMEM(weight.shape, jnp.float32),
            pltpu.VMEM((run, LANES), jnp.float32),
            pltpu.VMEM((run, LANES), jnp.float32),
            pltpu.SemaphoreType.DMA((2 + blocks * (rows // SUB) * PARTS,)),
        ],
        compiler_params=PARAMS,
    )(squares, *ready, moments[0])
    return new_weight, one.reshape(moment_one.shape), two.reshape(moment_two.shape)


def solution(mesh):
    return jax.shard_map(
        on_device,
        mesh=mesh,
        in_specs=(
            P("rep", "shard", None, None),
            P("shard", None, None),
            P("shard", "rep", None),
            P("shard", "rep", None),
        ),
        out_specs=(P("shard", None, None), P("shard", "rep", None), P("shard", "rep", None)),
        check_vma=False,
    )
```

```python
import functools
import operator

import jax
import jax.numpy as jnp
from jax import lax
from jax.experimental import pallas as pl
from jax.experimental.pallas import tpu as pltpu
from jax.sharding import PartitionSpec as P

STEP = 100
LANES = 128
PARTS = 4
SUB = 8
VMEM = pl.BlockSpec(memory_space=pltpu.VMEM)
SMEM = pl.BlockSpec(memory_space=pltpu.SMEM)
PARAMS = pltpu.CompilerParams(vmem_limit_bytes=32 << 20)


def f32(*shape):
    return jax.ShapeDtypeStruct(shape, jnp.float32)


def middle_sum(values, trim):
    low, high, total = [], [], None
    for value in values:
        for place in reversed(range(len(low))):
            low[place], value = jnp.minimum(low[place], value), jnp.maximum(low[place], value)
        if len(low) < trim:
            low.append(value)
            continue
        for place in range(len(high)):
            value, high[place] = jnp.minimum(high[place], value), jnp.maximum(high[place], value)
        if len(high) < trim:
            high.insert(0, value)
            continue
        total = value if total is None else total + value
    return total


def trim_kernel(trim, received_ref, trimmed_ref):
    count, tiles = received_ref.shape[:2]
    for tile in range(tiles):
        values = [received_ref[i, tile] for i in range(count)]
        mean = middle_sum(values, trim) / (count - 2 * trim)
        for i in range(count):
            trimmed_ref[i, tile] = mean


def square_kernel(trimmed_ref, squares_ref):
    squares = jnp.zeros((SUB, LANES), jnp.float32)
    for owner in range(trimmed_ref.shape[0]):
        for tile in range(trimmed_ref.shape[1]):
            squares += trimmed_ref[owner, tile] * trimmed_ref[owner, tile]
    squares_ref[...] = squares


def ready_kernel(shards, orders, at_ref, weight_ref, trimmed_ref, *refs):
    moment_refs, (kept_ref, one_ref, one_slope_ref, two_ref, two_slope_ref, own_ref, moments) = refs[: len(orders)], refs[len(orders) :]
    blocks, rows, cols = weight_ref.shape
    across = cols // LANES
    run = blocks * across
    me, core = at_ref[0] // shards, at_ref[0] % 2
    for order, ref in zip(orders, moment_refs):
        for part, place in enumerate(order):
            away = jnp.where(core == 0, place[0], place[1])
            row = pl.multiple_of((me ^ away) * 2 * run, 2 * run)
            moments[pl.ds(row, 2 * run), :] = ref[part * 2 * run : (part + 1) * 2 * run, :]
    start = (me // SUB) * across * SUB + me % SUB
    for b in range(blocks):
        base = b * (rows // SUB) * across * SUB
        own_ref[b * across : (b + 1) * across, :] = trimmed_ref[pl.ds(base + start, across, stride=SUB), :]
    one_scale, two_scale = 0.05 / (1.0 - 0.9**STEP), 1.0 / (1.0 - 0.95**STEP)
    at = 0
    for b in range(blocks):
        for r in range(0, rows, SUB):
            for j in range(across):
                col = b * across + j
                tile = slice(at, at + SUB)
                trimmed = trimmed_ref[tile, :]
                one = moments[pl.ds(2 * r * run + col, SUB, stride=2 * run), :]
                two = moments[pl.ds((2 * r + 1) * run + col, SUB, stride=2 * run), :]
                weight = weight_ref[b, r : r + SUB, j * LANES : (j + 1) * LANES]
                kept_ref[tile, :] = weight - 0.05 * (0.1 * weight)
                one_ref[tile, :] = (0.9 * one_scale) * one
                one_slope_ref[tile, :] = (0.1 * one_scale) * trimmed
                two_ref[tile, :] = (0.95 * two_scale) * two
                two_slope_ref[tile, :] = (0.05 * two_scale) * trimmed * trimmed
                at += SUB


def adam_kernel(params, squares_ref, kept_ref, one_ref, one_slope_ref, two_ref, two_slope_ref, own_ref, own_moments_ref, *refs):
    outs, stages, done = refs[:3], refs[3:6], refs[6]
    new, new_one, new_two = stages
    total = jnp.sum(squares_ref[...], keepdims=True)
    factor = jnp.minimum(1.0, 1.0 / jnp.sqrt(total / params + 1e-12))
    square = factor * factor
    run = own_ref.shape[0]
    clipped = factor * own_ref[...]
    new_one[...] = 0.9 * own_moments_ref[0:run, :] + 0.1 * clipped
    new_two[...] = 0.95 * own_moments_ref[run : 2 * run, :] + 0.05 * clipped * clipped
    copies = [pltpu.make_async_copy(new_one, outs[1], done.at[0]), pltpu.make_async_copy(new_two, outs[2], done.at[1])]
    for copy in copies:
        copy.start()
    blocks, rows, cols = new.shape
    across = cols // LANES
    at = 0
    for b in range(blocks):
        for r in range(0, rows, SUB):
            for j in range(across):
                tile = slice(at, at + SUB)
                one = one_ref[tile, :] + factor * one_slope_ref[tile, :]
                two = two_ref[tile, :] + square * two_slope_ref[tile, :]
                new[b, r : r + SUB, j * LANES : (j + 1) * LANES] = kept_ref[tile, :] - one / (jnp.sqrt(two) + 1e-08)
                at += SUB
                if (j + 1) % (across // PARTS) == 0:
                    part = slice((j + 1 - across // PARTS) * LANES, (j + 1) * LANES)
                    place = (b, slice(r, r + SUB), part)
                    copies.append(pltpu.make_async_copy(new.at[place], outs[0].at[place], done.at[len(copies)]))
                    copies[-1].start()
    for copy in copies:
        copy.wait()


def from_middle(count):
    return sorted(range(count), key=lambda i: (i % 2, abs(40 * (i // 2) - (19 + 2 * (i % 2)) * (count // 2))))


def on_device(grads, weight, moment_one, moment_two):
    count, shards = lax.axis_size("rep"), lax.axis_size("shard")
    blocks, rows, cols = weight.shape
    params = blocks * shards * rows * cols
    run = blocks * cols // LANES
    tiles = blocks * rows * cols // (SUB * LANES) // count

    def swap(value, axis, mask):
        return lax.ppermute(value, axis, [(i, i ^ mask) for i in range(lax.axis_size(axis))])

    order = from_middle(count)
    tiled = grads.reshape(blocks, rows // SUB, SUB, cols // LANES, LANES).transpose(0, 1, 3, 2, 4)
    received = lax.all_to_all(tiled.reshape(count, tiles, SUB, LANES), "rep", 0, 0, tiled=True, axis_index_groups=[order])

    moments = [jnp.concatenate([moment_one.reshape(run, LANES), moment_two.reshape(run, LANES)])]
    orders = [[(0, 0)]]
    masks = list(zip([1, 6, 2], [2, 6, 1]))

    def spread(mask):
        held = moments[0] if len(moments) == 1 else jnp.concatenate(moments)
        orders.append([tuple(map(operator.xor, place, mask)) for order in orders for place in order])
        pairs = [(r * shards + s, (r ^ mask[s % 2]) * shards + s) for r in range(count) for s in range(shards)]
        moments.append(lax.ppermute(held, ("rep", "shard"), pairs))

    for mask in masks:
        spread(mask)
    trimmed = pl.pallas_call(
        functools.partial(trim_kernel, count // 8),
        out_shape=f32(count, tiles, SUB, LANES),
        in_specs=[VMEM],
        out_specs=VMEM,
        compiler_params=PARAMS,
    )(received)
    trimmed = lax.all_to_all(trimmed, "rep", 0, 0, tiled=True, axis_index_groups=[order])
    squares = pl.pallas_call(
        square_kernel, out_shape=f32(SUB, LANES), in_specs=[VMEM], out_specs=VMEM, compiler_params=PARAMS
    )(trimmed)
    for mask in [1] + [(1 << bit) + 1 for bit in range(1, (shards - 1).bit_length())]:
        squares += swap(squares, "shard", mask)
    at = lax.axis_index(("rep", "shard")).reshape(1)
    flat = f32(weight.size // LANES, LANES)
    ready = pl.pallas_call(
        functools.partial(ready_kernel, shards, orders),
        out_shape=(flat,) * 5 + (f32(run, LANES),),
        in_specs=[SMEM] + [VMEM] * (2 + len(moments)),
        out_specs=(VMEM,) * 6,
        scratch_shapes=[pltpu.VMEM((count * 2 * run, LANES), jnp.float32)],
        compiler_params=PARAMS,
    )(at, weight, trimmed.reshape(-1, LANES), *moments)
    new_weight, one, two = pl.pallas_call(
        functools.partial(adam_kernel, params),
        out_shape=(f32(*weight.shape), f32(run, LANES), f32(run, LANES)),
        in_specs=[VMEM] * 8,
        out_specs=(pl.BlockSpec(memory_space=pl.ANY),) * 3,
        scratch_shapes=[
            pltpu.VMEM(weight.shape, jnp.float32),
            pltpu.VMEM((run, LANES), jnp.float32),
            pltpu.VMEM((run, LANES), jnp.float32),
            pltpu.SemaphoreType.DMA((2 + blocks * (rows // SUB) * PARTS,)),
        ],
        compiler_params=PARAMS,
    )(squares, *ready, moments[0])
    return new_weight, one.reshape(moment_one.shape), two.reshape(moment_two.shape)


def solution(mesh):
    return jax.shard_map(
        on_device,
        mesh=mesh,
        in_specs=(
            P("rep", "shard", None, None),
            P("shard", None, None),
            P("shard", "rep", None),
            P("shard", "rep", None),
        ),
        out_specs=(P("shard", None, None), P("shard", "rep", None), P("shard", "rep", None)),
        check_vma=False,
    )
```

```python
import functools
import operator

import jax
import jax.numpy as jnp
from jax import lax
from jax.experimental import pallas as pl
from jax.experimental.pallas import tpu as pltpu
from jax.sharding import PartitionSpec as P

STEP = 100
LANES = 128
PARTS = 4
SUB = 8
VMEM = pl.BlockSpec(memory_space=pltpu.VMEM)
SMEM = pl.BlockSpec(memory_space=pltpu.SMEM)
PARAMS = pltpu.CompilerParams(vmem_limit_bytes=32 << 20)


def f32(*shape):
    return jax.ShapeDtypeStruct(shape, jnp.float32)


def middle_sum(values, trim):
    low, high, total = [], [], None
    for value in values:
        for place in reversed(range(len(low))):
            low[place], value = jnp.minimum(low[place], value), jnp.maximum(low[place], value)
        if len(low) < trim:
            low.append(value)
            continue
        for place in range(len(high)):
            value, high[place] = jnp.minimum(high[place], value), jnp.maximum(high[place], value)
        if len(high) < trim:
            high.insert(0, value)
            continue
        total = value if total is None else total + value
    return total


def trim_kernel(trim, received_ref, trimmed_ref):
    count, tiles = received_ref.shape[:2]
    for tile in range(tiles):
        values = [received_ref[i, tile] for i in range(count)]
        mean = middle_sum(values, trim) / (count - 2 * trim)
        for i in range(count):
            trimmed_ref[i, tile] = mean


def square_kernel(trimmed_ref, squares_ref):
    squares = jnp.zeros((SUB, LANES), jnp.float32)
    for owner in range(trimmed_ref.shape[0]):
        for tile in range(trimmed_ref.shape[1]):
            squares += trimmed_ref[owner, tile] * trimmed_ref[owner, tile]
    squares_ref[...] = squares


def ready_kernel(shards, orders, at_ref, weight_ref, trimmed_ref, *refs):
    moment_refs, (kept_ref, one_ref, one_slope_ref, two_ref, two_slope_ref, own_ref, moments) = refs[: len(orders)], refs[len(orders) :]
    blocks, rows, cols = weight_ref.shape
    across = cols // LANES
    run = blocks * across
    me, core = at_ref[0] // shards, at_ref[0] % 2
    for order, ref in zip(orders, moment_refs):
        for part, place in enumerate(order):
            away = jnp.where(core == 0, place[0], place[1])
            row = pl.multiple_of((me ^ away) * 2 * run, 2 * run)
            moments[pl.ds(row, 2 * run), :] = ref[part * 2 * run : (part + 1) * 2 * run, :]
    start = (me // SUB) * across * SUB + me % SUB
    for b in range(blocks):
        base = b * (rows // SUB) * across * SUB
        own_ref[b * across : (b + 1) * across, :] = trimmed_ref[pl.ds(base + start, across, stride=SUB), :]
    one_scale, two_scale = 0.05 / (1.0 - 0.9**STEP), 1.0 / (1.0 - 0.95**STEP)
    at = 0
    for b in range(blocks):
        for r in range(0, rows, SUB):
            for j in range(across):
                col = b * across + j
                tile = slice(at, at + SUB)
                trimmed = trimmed_ref[tile, :]
                one = moments[pl.ds(2 * r * run + col, SUB, stride=2 * run), :]
                two = moments[pl.ds((2 * r + 1) * run + col, SUB, stride=2 * run), :]
                weight = weight_ref[b, r : r + SUB, j * LANES : (j + 1) * LANES]
                kept_ref[tile, :] = weight - 0.05 * (0.1 * weight)
                one_ref[tile, :] = (0.9 * one_scale) * one
                one_slope_ref[tile, :] = (0.1 * one_scale) * trimmed
                two_ref[tile, :] = (0.95 * two_scale) * two
                two_slope_ref[tile, :] = (0.05 * two_scale) * trimmed * trimmed
                at += SUB


def adam_kernel(params, squares_ref, kept_ref, one_ref, one_slope_ref, two_ref, two_slope_ref, own_ref, own_moments_ref, *refs):
    outs, stages, done = refs[:3], refs[3:6], refs[6]
    new, new_one, new_two = stages
    total = jnp.sum(squares_ref[...], keepdims=True)
    factor = jnp.minimum(1.0, 1.0 / jnp.sqrt(total / params + 1e-12))
    square = factor * factor
    run = own_ref.shape[0]
    clipped = factor * own_ref[...]
    new_one[...] = 0.9 * own_moments_ref[0:run, :] + 0.1 * clipped
    new_two[...] = 0.95 * own_moments_ref[run : 2 * run, :] + 0.05 * clipped * clipped
    copies = [pltpu.make_async_copy(new_one, outs[1], done.at[0]), pltpu.make_async_copy(new_two, outs[2], done.at[1])]
    for copy in copies:
        copy.start()
    blocks, rows, cols = new.shape
    across = cols // LANES
    at = 0
    for b in range(blocks):
        for r in range(0, rows, SUB):
            for j in range(across):
                tile = slice(at, at + SUB)
                one = one_ref[tile, :] + factor * one_slope_ref[tile, :]
                two = two_ref[tile, :] + square * two_slope_ref[tile, :]
                new[b, r : r + SUB, j * LANES : (j + 1) * LANES] = kept_ref[tile, :] - one / (jnp.sqrt(two) + 1e-08)
                at += SUB
                if (j + 1) % (across // PARTS) == 0:
                    part = slice((j + 1 - across // PARTS) * LANES, (j + 1) * LANES)
                    place = (b, slice(r, r + SUB), part)
                    copies.append(pltpu.make_async_copy(new.at[place], outs[0].at[place], done.at[len(copies)]))
                    copies[-1].start()
    for copy in copies:
        copy.wait()


def from_middle(count):
    return sorted(range(count), key=lambda i: (i % 2, abs(40 * (i // 2) - (19 + 2 * (i % 2)) * (count // 2))))


def on_device(grads, weight, moment_one, moment_two):
    count, shards = lax.axis_size("rep"), lax.axis_size("shard")
    blocks, rows, cols = weight.shape
    params = blocks * shards * rows * cols
    run = blocks * cols // LANES
    tiles = blocks * rows * cols // (SUB * LANES) // count

    def swap(value, axis, mask):
        return lax.ppermute(value, axis, [(i, i ^ mask) for i in range(lax.axis_size(axis))])

    order = from_middle(count)
    tiled = grads.reshape(blocks, rows // SUB, SUB, cols // LANES, LANES).transpose(0, 1, 3, 2, 4)
    received = lax.all_to_all(tiled.reshape(count, tiles, SUB, LANES), "rep", 0, 0, tiled=True, axis_index_groups=[order])

    moments = [jnp.concatenate([moment_one.reshape(run, LANES), moment_two.reshape(run, LANES)])]
    orders = [[(0, 0)]]
    middle = [3 << bit for bit in range(1, (count - 1).bit_length() - 1)]
    masks = list(zip([1, *middle, 2], [2, *middle, 1]))

    def spread(mask):
        held = moments[0] if len(moments) == 1 else jnp.concatenate(moments)
        orders.append([tuple(map(operator.xor, place, mask)) for order in orders for place in order])
        pairs = [(r * shards + s, (r ^ mask[s % 2]) * shards + s) for r in range(count) for s in range(shards)]
        moments.append(lax.ppermute(held, ("rep", "shard"), pairs))

    for mask in masks:
        spread(mask)
    trimmed = pl.pallas_call(
        functools.partial(trim_kernel, count // 8),
        out_shape=f32(count, tiles, SUB, LANES),
        in_specs=[VMEM],
        out_specs=VMEM,
        compiler_params=PARAMS,
    )(received)
    trimmed = lax.all_to_all(trimmed, "rep", 0, 0, tiled=True, axis_index_groups=[order])
    squares = pl.pallas_call(
        square_kernel, out_shape=f32(SUB, LANES), in_specs=[VMEM], out_specs=VMEM, compiler_params=PARAMS
    )(trimmed)
    for mask in [1] + [(1 << bit) + 1 for bit in range(1, (shards - 1).bit_length())]:
        squares += swap(squares, "shard", mask)
    at = lax.axis_index(("rep", "shard")).reshape(1)
    flat = f32(weight.size // LANES, LANES)
    ready = pl.pallas_call(
        functools.partial(ready_kernel, shards, orders),
        out_shape=(flat,) * 5 + (f32(run, LANES),),
        in_specs=[SMEM] + [VMEM] * (2 + len(moments)),
        out_specs=(VMEM,) * 6,
        scratch_shapes=[pltpu.VMEM((count * 2 * run, LANES), jnp.float32)],
        compiler_params=PARAMS,
    )(at, weight, trimmed.reshape(-1, LANES), *moments)
    new_weight, one, two = pl.pallas_call(
        functools.partial(adam_kernel, params),
        out_shape=(f32(*weight.shape), f32(run, LANES), f32(run, LANES)),
        in_specs=[VMEM] * 8,
        out_specs=(pl.BlockSpec(memory_space=pl.ANY),) * 3,
        scratch_shapes=[
            pltpu.VMEM(weight.shape, jnp.float32),
            pltpu.VMEM((run, LANES), jnp.float32),
            pltpu.VMEM((run, LANES), jnp.float32),
            pltpu.SemaphoreType.DMA((2 + blocks * (rows // SUB) * PARTS,)),
        ],
        compiler_params=PARAMS,
    )(squares, *ready, moments[0])
    return new_weight, one.reshape(moment_one.shape), two.reshape(moment_two.shape)


def solution(mesh):
    return jax.shard_map(
        on_device,
        mesh=mesh,
        in_specs=(
            P("rep", "shard", None, None),
            P("shard", None, None),
            P("shard", "rep", None),
            P("shard", "rep", None),
        ),
        out_specs=(P("shard", None, None), P("shard", "rep", None), P("shard", "rep", None)),
        check_vma=False,
    )
```

```python
import functools
import operator

import jax
import jax.numpy as jnp
from jax import lax
from jax.experimental import pallas as pl
from jax.experimental.pallas import tpu as pltpu
from jax.sharding import PartitionSpec as P

STEP = 100
LANES = 128
PARTS = 4
SUB = 8
VMEM = pl.BlockSpec(memory_space=pltpu.VMEM)
SMEM = pl.BlockSpec(memory_space=pltpu.SMEM)
PARAMS = pltpu.CompilerParams(vmem_limit_bytes=32 << 20)


def f32(*shape):
    return jax.ShapeDtypeStruct(shape, jnp.float32)


def middle_sum(values, trim):
    low, high, total = [], [], None
    for value in values:
        for place in reversed(range(len(low))):
            low[place], value = jnp.minimum(low[place], value), jnp.maximum(low[place], value)
        if len(low) < trim:
            low.append(value)
            continue
        for place in range(len(high)):
            value, high[place] = jnp.minimum(high[place], value), jnp.maximum(high[place], value)
        if len(high) < trim:
            high.insert(0, value)
            continue
        total = value if total is None else total + value
    return total


def trim_kernel(trim, received_ref, trimmed_ref, mean_ref, done):
    count, tiles = received_ref.shape[:2]
    copies = []
    for first, last in ((0, tiles // 2), (tiles // 2, tiles)):
        for tile in range(first, last):
            values = [received_ref[i, tile] for i in range(count)]
            mean_ref[tile] = middle_sum(values, trim) / (count - 2 * trim)
        part = slice(first, last)
        for i in range(count):
            copies.append(pltpu.make_async_copy(mean_ref.at[part], trimmed_ref.at[i, part], done.at[len(copies)]))
            copies[-1].start()
    for copy in copies:
        copy.wait()


def square_kernel(trimmed_ref, squares_ref):
    squares = jnp.zeros((SUB, LANES), jnp.float32)
    for owner in range(trimmed_ref.shape[0]):
        for tile in range(trimmed_ref.shape[1]):
            squares += trimmed_ref[owner, tile] * trimmed_ref[owner, tile]
    squares_ref[...] = squares


def ready_kernel(shards, orders, at_ref, weight_ref, trimmed_ref, *refs):
    moment_refs, (kept_ref, one_ref, one_slope_ref, two_ref, two_slope_ref, own_ref, moments) = refs[: len(orders)], refs[len(orders) :]
    blocks, rows, cols = weight_ref.shape
    across = cols // LANES
    run = blocks * across
    me, core = at_ref[0] // shards, at_ref[0] % 2
    for order, ref in zip(orders, moment_refs):
        for part, place in enumerate(order):
            away = jnp.where(core == 0, place[0], place[1])
            row = pl.multiple_of((me ^ away) * 2 * run, 2 * run)
            moments[pl.ds(row, 2 * run), :] = ref[part * 2 * run : (part + 1) * 2 * run, :]
    start = (me // SUB) * across * SUB + me % SUB
    for b in range(blocks):
        base = b * (rows // SUB) * across * SUB
        own_ref[b * across : (b + 1) * across, :] = trimmed_ref[pl.ds(base + start, across, stride=SUB), :]
    one_scale, two_scale = 0.05 / (1.0 - 0.9**STEP), 1.0 / (1.0 - 0.95**STEP)
    at = 0
    for b in range(blocks):
        for r in range(0, rows, SUB):
            for j in range(across):
                col = b * across + j
                tile = slice(at, at + SUB)
                trimmed = trimmed_ref[tile, :]
                one = moments[pl.ds(2 * r * run + col, SUB, stride=2 * run), :]
                two = moments[pl.ds((2 * r + 1) * run + col, SUB, stride=2 * run), :]
                weight = weight_ref[b, r : r + SUB, j * LANES : (j + 1) * LANES]
                kept_ref[tile, :] = weight - 0.05 * (0.1 * weight)
                one_ref[tile, :] = (0.9 * one_scale) * one
                one_slope_ref[tile, :] = (0.1 * one_scale) * trimmed
                two_ref[tile, :] = (0.95 * two_scale) * two
                two_slope_ref[tile, :] = (0.05 * two_scale) * trimmed * trimmed
                at += SUB


def adam_kernel(params, squares_ref, kept_ref, one_ref, one_slope_ref, two_ref, two_slope_ref, own_ref, own_moments_ref, *refs):
    outs, stages, done = refs[:3], refs[3:6], refs[6]
    new, new_one, new_two = stages
    total = jnp.sum(squares_ref[...], keepdims=True)
    factor = jnp.minimum(1.0, 1.0 / jnp.sqrt(total / params + 1e-12))
    square = factor * factor
    run = own_ref.shape[0]
    clipped = factor * own_ref[...]
    new_one[...] = 0.9 * own_moments_ref[0:run, :] + 0.1 * clipped
    new_two[...] = 0.95 * own_moments_ref[run : 2 * run, :] + 0.05 * clipped * clipped
    copies = [pltpu.make_async_copy(new_one, outs[1], done.at[0]), pltpu.make_async_copy(new_two, outs[2], done.at[1])]
    for copy in copies:
        copy.start()
    blocks, rows, cols = new.shape
    across = cols // LANES
    at = 0
    for b in range(blocks):
        for r in range(0, rows, SUB):
            for j in range(across):
                tile = slice(at, at + SUB)
                one = one_ref[tile, :] + factor * one_slope_ref[tile, :]
                two = two_ref[tile, :] + square * two_slope_ref[tile, :]
                new[b, r : r + SUB, j * LANES : (j + 1) * LANES] = kept_ref[tile, :] - one / (jnp.sqrt(two) + 1e-08)
                at += SUB
                if (j + 1) % (across // PARTS) == 0:
                    part = slice((j + 1 - across // PARTS) * LANES, (j + 1) * LANES)
                    place = (b, slice(r, r + SUB), part)
                    copies.append(pltpu.make_async_copy(new.at[place], outs[0].at[place], done.at[len(copies)]))
                    copies[-1].start()
    for copy in copies:
        copy.wait()


def from_middle(count):
    return sorted(range(count), key=lambda i: (i % 2, abs(40 * (i // 2) - (19 + 2 * (i % 2)) * (count // 2))))


def on_device(grads, weight, moment_one, moment_two):
    count, shards = lax.axis_size("rep"), lax.axis_size("shard")
    blocks, rows, cols = weight.shape
    params = blocks * shards * rows * cols
    run = blocks * cols // LANES
    tiles = blocks * rows * cols // (SUB * LANES) // count

    def swap(value, axis, mask):
        return lax.ppermute(value, axis, [(i, i ^ mask) for i in range(lax.axis_size(axis))])

    order = from_middle(count)
    tiled = grads.reshape(blocks, rows // SUB, SUB, cols // LANES, LANES).transpose(0, 1, 3, 2, 4)
    received = lax.all_to_all(tiled.reshape(count, tiles, SUB, LANES), "rep", 0, 0, tiled=True, axis_index_groups=[order])

    moments = [jnp.concatenate([moment_one.reshape(run, LANES), moment_two.reshape(run, LANES)])]
    orders = [[(0, 0)]]
    middle = [3 << bit for bit in range(1, (count - 1).bit_length() - 1)]
    masks = list(zip([1, *middle, 2], [2, *middle, 1]))

    def spread(mask):
        held = moments[0] if len(moments) == 1 else jnp.concatenate(moments)
        orders.append([tuple(map(operator.xor, place, mask)) for order in orders for place in order])
        pairs = [(r * shards + s, (r ^ mask[s % 2]) * shards + s) for r in range(count) for s in range(shards)]
        moments.append(lax.ppermute(held, ("rep", "shard"), pairs))

    for mask in masks:
        spread(mask)
    trimmed = pl.pallas_call(
        functools.partial(trim_kernel, count // 8),
        out_shape=f32(count, tiles, SUB, LANES),
        in_specs=[VMEM],
        out_specs=pl.BlockSpec(memory_space=pl.ANY),
        scratch_shapes=[pltpu.VMEM((tiles, SUB, LANES), jnp.float32), pltpu.SemaphoreType.DMA((2 * count,))],
        compiler_params=PARAMS,
    )(received)
    trimmed = lax.all_to_all(trimmed, "rep", 0, 0, tiled=True, axis_index_groups=[order])
    squares = pl.pallas_call(
        square_kernel, out_shape=f32(SUB, LANES), in_specs=[VMEM], out_specs=VMEM, compiler_params=PARAMS
    )(trimmed)
    for mask in [(1 << bit) + 1 for bit in range(1, (shards - 1).bit_length())] + [1]:
        squares += swap(squares, "shard", mask)
    at = lax.axis_index(("rep", "shard")).reshape(1)
    flat = f32(weight.size // LANES, LANES)
    ready = pl.pallas_call(
        functools.partial(ready_kernel, shards, orders),
        out_shape=(flat,) * 5 + (f32(run, LANES),),
        in_specs=[SMEM] + [VMEM] * (2 + len(moments)),
        out_specs=(VMEM,) * 6,
        scratch_shapes=[pltpu.VMEM((count * 2 * run, LANES), jnp.float32)],
        compiler_params=PARAMS,
    )(at, weight, trimmed.reshape(-1, LANES), *moments)
    new_weight, one, two = pl.pallas_call(
        functools.partial(adam_kernel, params),
        out_shape=(f32(*weight.shape), f32(run, LANES), f32(run, LANES)),
        in_specs=[VMEM] * 8,
        out_specs=(pl.BlockSpec(memory_space=pl.ANY),) * 3,
        scratch_shapes=[
            pltpu.VMEM(weight.shape, jnp.float32),
            pltpu.VMEM((run, LANES), jnp.float32),
            pltpu.VMEM((run, LANES), jnp.float32),
            pltpu.SemaphoreType.DMA((2 + blocks * (rows // SUB) * PARTS,)),
        ],
        compiler_params=PARAMS,
    )(squares, *ready, moments[0])
    return new_weight, one.reshape(moment_one.shape), two.reshape(moment_two.shape)


def solution(mesh):
    return jax.shard_map(
        on_device,
        mesh=mesh,
        in_specs=(
            P("rep", "shard", None, None),
            P("shard", None, None),
            P("shard", "rep", None),
            P("shard", "rep", None),
        ),
        out_specs=(P("shard", None, None), P("shard", "rep", None), P("shard", "rep", None)),
        check_vma=False,
    )
```

```python
import functools
import operator

import jax
import jax.numpy as jnp
from jax import lax
from jax.experimental import pallas as pl
from jax.experimental.pallas import tpu as pltpu
from jax.sharding import PartitionSpec as P

STEP = 100
LANES = 128
PARTS = 4
SUB = 8
VMEM = pl.BlockSpec(memory_space=pltpu.VMEM)
SMEM = pl.BlockSpec(memory_space=pltpu.SMEM)
PARAMS = pltpu.CompilerParams(vmem_limit_bytes=32 << 20)


def f32(*shape):
    return jax.ShapeDtypeStruct(shape, jnp.float32)


def middle_sum(values, trim):
    low, high, total = [], [], None
    for value in values:
        for place in reversed(range(len(low))):
            low[place], value = jnp.minimum(low[place], value), jnp.maximum(low[place], value)
        if len(low) < trim:
            low.append(value)
            continue
        for place in range(len(high)):
            value, high[place] = jnp.minimum(high[place], value), jnp.maximum(high[place], value)
        if len(high) < trim:
            high.insert(0, value)
            continue
        total = value if total is None else total + value
    return total


def trim_kernel(trim, received_ref, trimmed_ref):
    count, tiles = received_ref.shape[:2]
    for tile in range(tiles):
        values = [received_ref[i, tile] for i in range(count)]
        mean = middle_sum(values, trim) / (count - 2 * trim)
        for i in range(count):
            trimmed_ref[i, tile] = mean


def square_kernel(trimmed_ref, squares_ref):
    squares = jnp.zeros((SUB, LANES), jnp.float32)
    for owner in range(trimmed_ref.shape[0]):
        for tile in range(trimmed_ref.shape[1]):
            squares += trimmed_ref[owner, tile] * trimmed_ref[owner, tile]
    squares_ref[...] = squares


def ready_kernel(shards, orders, at_ref, weight_ref, trimmed_ref, *refs):
    moment_refs, (kept_ref, one_ref, one_slope_ref, two_ref, two_slope_ref, own_ref, moments) = refs[: len(orders)], refs[len(orders) :]
    blocks, rows, cols = weight_ref.shape
    across = cols // LANES
    run = blocks * across
    me, core = at_ref[0] // shards, at_ref[0] % 2
    for order, ref in zip(orders, moment_refs):
        for part, place in enumerate(order):
            away = jnp.where(core == 0, place[0], place[1])
            row = pl.multiple_of((me ^ away) * 2 * run, 2 * run)
            moments[pl.ds(row, 2 * run), :] = ref[part * 2 * run : (part + 1) * 2 * run, :]
    start = (me // SUB) * across * SUB + me % SUB
    for b in range(blocks):
        base = b * (rows // SUB) * across * SUB
        own_ref[b * across : (b + 1) * across, :] = trimmed_ref[pl.ds(base + start, across, stride=SUB), :]
    one_scale, two_scale = 0.05 / (1.0 - 0.9**STEP), 1.0 / (1.0 - 0.95**STEP)
    at = 0
    for b in range(blocks):
        for r in range(0, rows, SUB):
            for j in range(across):
                col = b * across + j
                tile = slice(at, at + SUB)
                trimmed = trimmed_ref[tile, :]
                one = moments[pl.ds(2 * r * run + col, SUB, stride=2 * run), :]
                two = moments[pl.ds((2 * r + 1) * run + col, SUB, stride=2 * run), :]
                weight = weight_ref[b, r : r + SUB, j * LANES : (j + 1) * LANES]
                kept_ref[tile, :] = weight - 0.05 * (0.1 * weight)
                one_ref[tile, :] = (0.9 * one_scale) * one
                one_slope_ref[tile, :] = (0.1 * one_scale) * trimmed
                two_ref[tile, :] = (0.95 * two_scale) * two
                two_slope_ref[tile, :] = (0.05 * two_scale) * trimmed * trimmed
                at += SUB


def adam_kernel(params, squares_ref, others_ref, kept_ref, one_ref, one_slope_ref, two_ref, two_slope_ref, own_ref, own_moments_ref, *refs):
    outs, stages, done = refs[:3], refs[3:6], refs[6]
    new, new_one, new_two = stages
    total = jnp.sum(squares_ref[...] + others_ref[...], keepdims=True)
    factor = jnp.minimum(1.0, 1.0 / jnp.sqrt(total / params + 1e-12))
    square = factor * factor
    run = own_ref.shape[0]
    clipped = factor * own_ref[...]
    new_one[...] = 0.9 * own_moments_ref[0:run, :] + 0.1 * clipped
    new_two[...] = 0.95 * own_moments_ref[run : 2 * run, :] + 0.05 * clipped * clipped
    copies = [pltpu.make_async_copy(new_one, outs[1], done.at[0]), pltpu.make_async_copy(new_two, outs[2], done.at[1])]
    for copy in copies:
        copy.start()
    blocks, rows, cols = new.shape
    across = cols // LANES
    at = 0
    for b in range(blocks):
        for r in range(0, rows, SUB):
            for j in range(across):
                tile = slice(at, at + SUB)
                one = one_ref[tile, :] + factor * one_slope_ref[tile, :]
                two = two_ref[tile, :] + square * two_slope_ref[tile, :]
                new[b, r : r + SUB, j * LANES : (j + 1) * LANES] = kept_ref[tile, :] - one / (jnp.sqrt(two) + 1e-08)
                at += SUB
                if (j + 1) % (across // PARTS) == 0:
                    part = slice((j + 1 - across // PARTS) * LANES, (j + 1) * LANES)
                    place = (b, slice(r, r + SUB), part)
                    copies.append(pltpu.make_async_copy(new.at[place], outs[0].at[place], done.at[len(copies)]))
                    copies[-1].start()
    for copy in copies:
        copy.wait()


def from_middle(count):
    return sorted(range(count), key=lambda i: (i % 2, abs(40 * (i // 2) - (19 + 2 * (i % 2)) * (count // 2))))


def on_device(grads, weight, moment_one, moment_two):
    count, shards = lax.axis_size("rep"), lax.axis_size("shard")
    blocks, rows, cols = weight.shape
    params = blocks * shards * rows * cols
    run = blocks * cols // LANES
    tiles = blocks * rows * cols // (SUB * LANES) // count

    def swap(value, axis, mask):
        return lax.ppermute(value, axis, [(i, i ^ mask) for i in range(lax.axis_size(axis))])

    order = from_middle(count)
    tiled = grads.reshape(blocks, rows // SUB, SUB, cols // LANES, LANES).transpose(0, 1, 3, 2, 4)
    received = lax.all_to_all(tiled.reshape(count, tiles, SUB, LANES), "rep", 0, 0, tiled=True, axis_index_groups=[order])

    moments = [jnp.concatenate([moment_one.reshape(run, LANES), moment_two.reshape(run, LANES)])]
    orders = [[(0, 0)]]
    middle = [3 << bit for bit in range(1, (count - 1).bit_length() - 1)]
    masks = list(zip([1, *middle, 2], [2, *middle, 1]))

    def spread(mask):
        held = moments[0] if len(moments) == 1 else jnp.concatenate(moments)
        orders.append([tuple(map(operator.xor, place, mask)) for order in orders for place in order])
        pairs = [(r * shards + s, (r ^ mask[s % 2]) * shards + s) for r in range(count) for s in range(shards)]
        moments.append(lax.ppermute(held, ("rep", "shard"), pairs))

    for mask in masks:
        spread(mask)
    trimmed = pl.pallas_call(
        functools.partial(trim_kernel, count // 8),
        out_shape=f32(count, tiles, SUB, LANES),
        in_specs=[VMEM],
        out_specs=VMEM,
        compiler_params=PARAMS,
    )(received)
    trimmed = lax.all_to_all(trimmed, "rep", 0, 0, tiled=True, axis_index_groups=[order])
    squares = pl.pallas_call(
        square_kernel, out_shape=f32(SUB, LANES), in_specs=[VMEM], out_specs=VMEM, compiler_params=PARAMS
    )(trimmed)
    others = jnp.zeros_like(squares)
    for mask in [1] + [(1 << bit) + 1 for bit in range(1, (shards - 1).bit_length())]:
        squares, others = squares + others, swap(squares + others, "shard", mask)
    at = lax.axis_index(("rep", "shard")).reshape(1)
    flat = f32(weight.size // LANES, LANES)
    ready = pl.pallas_call(
        functools.partial(ready_kernel, shards, orders),
        out_shape=(flat,) * 5 + (f32(run, LANES),),
        in_specs=[SMEM] + [VMEM] * (2 + len(moments)),
        out_specs=(VMEM,) * 6,
        scratch_shapes=[pltpu.VMEM((count * 2 * run, LANES), jnp.float32)],
        compiler_params=PARAMS,
    )(at, weight, trimmed.reshape(-1, LANES), *moments)
    new_weight, one, two = pl.pallas_call(
        functools.partial(adam_kernel, params),
        out_shape=(f32(*weight.shape), f32(run, LANES), f32(run, LANES)),
        in_specs=[VMEM] * 9,
        out_specs=(pl.BlockSpec(memory_space=pl.ANY),) * 3,
        scratch_shapes=[
            pltpu.VMEM(weight.shape, jnp.float32),
            pltpu.VMEM((run, LANES), jnp.float32),
            pltpu.VMEM((run, LANES), jnp.float32),
            pltpu.SemaphoreType.DMA((2 + blocks * (rows // SUB) * PARTS,)),
        ],
        compiler_params=PARAMS,
    )(squares, others, *ready, moments[0])
    return new_weight, one.reshape(moment_one.shape), two.reshape(moment_two.shape)


def solution(mesh):
    return jax.shard_map(
        on_device,
        mesh=mesh,
        in_specs=(
            P("rep", "shard", None, None),
            P("shard", None, None),
            P("shard", "rep", None),
            P("shard", "rep", None),
        ),
        out_specs=(P("shard", None, None), P("shard", "rep", None), P("shard", "rep", None)),
        check_vma=False,
    )
```

```python
import functools
import operator

import jax
import jax.numpy as jnp
from jax import lax
from jax.experimental import pallas as pl
from jax.experimental.pallas import tpu as pltpu
from jax.sharding import PartitionSpec as P

STEP = 100
LANES = 128
PARTS = 2
SUB = 8
VMEM = pl.BlockSpec(memory_space=pltpu.VMEM)
SMEM = pl.BlockSpec(memory_space=pltpu.SMEM)
PARAMS = pltpu.CompilerParams(vmem_limit_bytes=32 << 20)


def f32(*shape):
    return jax.ShapeDtypeStruct(shape, jnp.float32)


def middle_sum(values, trim):
    low, high, total = [], [], None
    for value in values:
        for place in reversed(range(len(low))):
            low[place], value = jnp.minimum(low[place], value), jnp.maximum(low[place], value)
        if len(low) < trim:
            low.append(value)
            continue
        for place in range(len(high)):
            value, high[place] = jnp.minimum(high[place], value), jnp.maximum(high[place], value)
        if len(high) < trim:
            high.insert(0, value)
            continue
        total = value if total is None else total + value
    return total


def trim_kernel(trim, received_ref, trimmed_ref):
    count, tiles = received_ref.shape[:2]
    for tile in range(tiles):
        values = [received_ref[i, tile] for i in range(count)]
        mean = middle_sum(values, trim) / (count - 2 * trim)
        for i in range(count):
            trimmed_ref[i, tile] = mean


def square_kernel(trimmed_ref, squares_ref):
    squares = jnp.zeros((SUB, LANES), jnp.float32)
    for owner in range(trimmed_ref.shape[0]):
        for tile in range(trimmed_ref.shape[1]):
            squares += trimmed_ref[owner, tile] * trimmed_ref[owner, tile]
    squares_ref[...] = squares


def ready_kernel(shards, orders, at_ref, weight_ref, trimmed_ref, *refs):
    moment_refs, (kept_ref, one_ref, one_slope_ref, two_ref, two_slope_ref, own_ref, moments) = refs[: len(orders)], refs[len(orders) :]
    blocks, rows, cols = weight_ref.shape
    across = cols // LANES
    run = blocks * across
    me, core = at_ref[0] // shards, at_ref[0] % 2
    for order, ref in zip(orders, moment_refs):
        for part, place in enumerate(order):
            away = jnp.where(core == 0, place[0], place[1])
            row = pl.multiple_of((me ^ away) * 2 * run, 2 * run)
            moments[pl.ds(row, 2 * run), :] = ref[part * 2 * run : (part + 1) * 2 * run, :]
    start = (me // SUB) * across * SUB + me % SUB
    for b in range(blocks):
        base = b * (rows // SUB) * across * SUB
        own_ref[b * across : (b + 1) * across, :] = trimmed_ref[pl.ds(base + start, across, stride=SUB), :]
    one_scale, two_scale = 0.05 / (1.0 - 0.9**STEP), 1.0 / (1.0 - 0.95**STEP)
    at = 0
    for b in range(blocks):
        for r in range(0, rows, SUB):
            for j in range(across):
                col = b * across + j
                tile = slice(at, at + SUB)
                trimmed = trimmed_ref[tile, :]
                one = moments[pl.ds(2 * r * run + col, SUB, stride=2 * run), :]
                two = moments[pl.ds((2 * r + 1) * run + col, SUB, stride=2 * run), :]
                weight = weight_ref[b, r : r + SUB, j * LANES : (j + 1) * LANES]
                kept_ref[tile, :] = weight - 0.05 * (0.1 * weight)
                one_ref[tile, :] = (0.9 * one_scale) * one
                one_slope_ref[tile, :] = (0.1 * one_scale) * trimmed
                two_ref[tile, :] = (0.95 * two_scale) * two
                two_slope_ref[tile, :] = (0.05 * two_scale) * trimmed * trimmed
                at += SUB


def adam_kernel(params, squares_ref, others_ref, kept_ref, one_ref, one_slope_ref, two_ref, two_slope_ref, own_ref, own_moments_ref, *refs):
    outs, stages, done = refs[:3], refs[3:6], refs[6]
    new, new_one, new_two = stages
    total = jnp.sum(squares_ref[...] + others_ref[...], keepdims=True)
    factor = jnp.minimum(1.0, 1.0 / jnp.sqrt(total / params + 1e-12))
    square = factor * factor
    run = own_ref.shape[0]
    clipped = factor * own_ref[...]
    new_one[...] = 0.9 * own_moments_ref[0:run, :] + 0.1 * clipped
    new_two[...] = 0.95 * own_moments_ref[run : 2 * run, :] + 0.05 * clipped * clipped
    copies = [pltpu.make_async_copy(new_one, outs[1], done.at[0]), pltpu.make_async_copy(new_two, outs[2], done.at[1])]
    for copy in copies:
        copy.start()
    blocks, rows, cols = new.shape
    across = cols // LANES
    at = 0
    for b in range(blocks):
        for r in range(0, rows, SUB):
            for j in range(across):
                tile = slice(at, at + SUB)
                one = one_ref[tile, :] + factor * one_slope_ref[tile, :]
                two = two_ref[tile, :] + square * two_slope_ref[tile, :]
                new[b, r : r + SUB, j * LANES : (j + 1) * LANES] = kept_ref[tile, :] - one / (jnp.sqrt(two) + 1e-08)
                at += SUB
                if (j + 1) % (across // PARTS) == 0:
                    part = slice((j + 1 - across // PARTS) * LANES, (j + 1) * LANES)
                    place = (b, slice(r, r + SUB), part)
                    copies.append(pltpu.make_async_copy(new.at[place], outs[0].at[place], done.at[len(copies)]))
                    copies[-1].start()
    for copy in copies:
        copy.wait()


def from_middle(count):
    return sorted(range(count), key=lambda i: (i % 2, abs(40 * (i // 2) - (19 + 2 * (i % 2)) * (count // 2))))


def on_device(grads, weight, moment_one, moment_two):
    count, shards = lax.axis_size("rep"), lax.axis_size("shard")
    blocks, rows, cols = weight.shape
    params = blocks * shards * rows * cols
    run = blocks * cols // LANES
    tiles = blocks * rows * cols // (SUB * LANES) // count

    def swap(value, axis, mask):
        return lax.ppermute(value, axis, [(i, i ^ mask) for i in range(lax.axis_size(axis))])

    order = from_middle(count)
    tiled = grads.reshape(blocks, rows // SUB, SUB, cols // LANES, LANES).transpose(0, 1, 3, 2, 4)
    received = lax.all_to_all(tiled.reshape(count, tiles, SUB, LANES), "rep", 0, 0, tiled=True, axis_index_groups=[order])

    moments = [jnp.concatenate([moment_one.reshape(run, LANES), moment_two.reshape(run, LANES)])]
    orders = [[(0, 0)]]
    middle = [3 << bit for bit in range(1, (count - 1).bit_length() - 1)]
    masks = list(zip([1, *middle, 2], [2, *middle, 1]))

    def spread(mask):
        held = moments[0] if len(moments) == 1 else jnp.concatenate(moments)
        orders.append([tuple(map(operator.xor, place, mask)) for order in orders for place in order])
        pairs = [(r * shards + s, (r ^ mask[s % 2]) * shards + s) for r in range(count) for s in range(shards)]
        moments.append(lax.ppermute(held, ("rep", "shard"), pairs))

    for mask in masks:
        spread(mask)
    trimmed = pl.pallas_call(
        functools.partial(trim_kernel, count // 8),
        out_shape=f32(count, tiles, SUB, LANES),
        in_specs=[VMEM],
        out_specs=VMEM,
        compiler_params=PARAMS,
    )(received)
    trimmed = lax.all_to_all(trimmed, "rep", 0, 0, tiled=True, axis_index_groups=[order])
    squares = pl.pallas_call(
        square_kernel, out_shape=f32(SUB, LANES), in_specs=[VMEM], out_specs=VMEM, compiler_params=PARAMS
    )(trimmed)
    others = jnp.zeros_like(squares)
    for mask in [1] + [(1 << bit) + 1 for bit in range(1, (shards - 1).bit_length())]:
        squares, others = squares + others, swap(squares + others, "shard", mask)
    at = lax.axis_index(("rep", "shard")).reshape(1)
    flat = f32(weight.size // LANES, LANES)
    ready = pl.pallas_call(
        functools.partial(ready_kernel, shards, orders),
        out_shape=(flat,) * 5 + (f32(run, LANES),),
        in_specs=[SMEM] + [VMEM] * (2 + len(moments)),
        out_specs=(VMEM,) * 6,
        scratch_shapes=[pltpu.VMEM((count * 2 * run, LANES), jnp.float32)],
        compiler_params=PARAMS,
    )(at, weight, trimmed.reshape(-1, LANES), *moments)
    new_weight, one, two = pl.pallas_call(
        functools.partial(adam_kernel, params),
        out_shape=(f32(*weight.shape), f32(run, LANES), f32(run, LANES)),
        in_specs=[VMEM] * 9,
        out_specs=(pl.BlockSpec(memory_space=pl.ANY),) * 3,
        scratch_shapes=[
            pltpu.VMEM(weight.shape, jnp.float32),
            pltpu.VMEM((run, LANES), jnp.float32),
            pltpu.VMEM((run, LANES), jnp.float32),
            pltpu.SemaphoreType.DMA((2 + blocks * (rows // SUB) * PARTS,)),
        ],
        compiler_params=PARAMS,
    )(squares, others, *ready, moments[0])
    return new_weight, one.reshape(moment_one.shape), two.reshape(moment_two.shape)


def solution(mesh):
    return jax.shard_map(
        on_device,
        mesh=mesh,
        in_specs=(
            P("rep", "shard", None, None),
            P("shard", None, None),
            P("shard", "rep", None),
            P("shard", "rep", None),
        ),
        out_specs=(P("shard", None, None), P("shard", "rep", None), P("shard", "rep", None)),
        check_vma=False,
    )
```
